128 devices in a mesh: row: 16 (over z, x_lo, core), col: 8 (over y, x_hi).
Axes of the slice: x: 4 (x_hi: 2, x_lo: 2; x = x_hi * 2 + x_lo), y: 4, z: 4, core: 2. Of those that a mesh axis runs over, the one named last changes fastest.
Arguments:
- image_emb: bfloat16 [16384, 1152], P(('row', 'col')), may hold values from -0.5 to 0.5, as said below
- text_emb: bfloat16 [16384, 1152], P(('col', 'row')), may hold values from -0.5 to 0.5, as said below
- scale: float32 [1], replicated, may hold values from 10 to 40
- bias: float32 [1], replicated, may hold values from -10 to -4
Outputs:
- grad_image: float32 [16384, 1152], P(('row', 'col'))
- grad_text: float32 [16384, 1152], P(('col', 'row'))
The draws below stay inside these ranges and needn't reach their ends.
Inputs may be any that keep to these rules, and one draw needn't show every extreme that they name: `image_emb`: raw tower outputs; the image and the text of the same index form a matching pair. `text_emb`: raw tower outputs, paired with image_emb by index.
All inputs are finite; a program needn't handle non-finite values.
Results may differ from the reference program's by a relative error of at most 0.0086.
Values may be sent and summed in bfloat16 or wider, within the bound.
A program may use at most 64 MiB of HBM per device.

```python
import math
import jax
import jax.numpy as jnp
from jax import lax

D = 1152
TOKENS = 16384
N_ROW = 16


def paired_base(key):
    base = jax.random.normal(key, (TOKENS, D), jnp.float32)
    return base


def draw_image_emb(key, part):
    base = paired_base(key)
    key = jax.random.fold_in(key, 3)
    noise = jax.random.normal(key, (TOKENS, D), jnp.float32)
    values = (base + 0.5 * noise) / jnp.sqrt(jnp.float32(D))
    return jnp.clip(values, -0.5, 0.5).astype(jnp.bfloat16)


def draw_text_emb(key, part):
    base = paired_base(key)
    key = jax.random.fold_in(key, 4)
    position = (jnp.arange(TOKENS, dtype=jnp.float32) / TOKENS).reshape(TOKENS, 1)
    level = 0.4 * jnp.exp(position * jnp.log(jnp.float32(5.0)))
    noise = jax.random.normal(key, (TOKENS, D), jnp.float32)
    values = (base + level * noise) / jnp.sqrt(jnp.float32(D))
    return jnp.clip(values, -0.5, 0.5).astype(jnp.bfloat16)


def setup_inputs(seed: int = 0) -> dict:
    seeds = jax.random.split(jax.random.key(seed), 5)
    image_emb = draw_image_emb(jax.random.fold_in(seeds[4], 71), 0)
    text_emb = draw_text_emb(jax.random.fold_in(seeds[4], 71), 0)
    scale = jnp.clip(jnp.exp(jax.random.uniform(seeds[2], (1,), jnp.float32, math.log(10.0), math.log(40.0))), 10.0, 40.0)
    bias = jnp.clip(jax.random.uniform(seeds[3], (1,), jnp.float32, -10.0, -4.0), -10.0, -4.0)
    return {"image_emb": image_emb, "text_emb": text_emb, "scale": scale, "bias": bias}


def unit_rows(raw):
    values = raw.astype(jnp.float32)
    inverse = lax.rsqrt(lax.optimization_barrier(jnp.sum(values * values, axis=1, keepdims=True)) + 1e-06)
    return (inverse, values * inverse)

def tile_terms(img_unit, txt_unit, img_start, txt_start, scale_value, bias_value):
    sims = lax.dot_general(img_unit, txt_unit, (((1,), (1,)), ((), ())), preferred_element_type=jnp.float32)
    logits = scale_value * sims + bias_value
    rows = img_start + lax.broadcasted_iota(jnp.int32, sims.shape, 0)
    cols = txt_start + lax.broadcasted_iota(jnp.int32, sims.shape, 1)
    sign = jnp.where(rows == cols, 1.0, -1.0).astype(jnp.float32)
    coef = (-scale_value * sign * jax.nn.sigmoid(-sign * logits)).astype(jnp.bfloat16)
    g_img = jnp.dot(coef, txt_unit, preferred_element_type=jnp.float32)
    g_txt = lax.dot_general(coef, img_unit, (((0,), (0,)), ((), ())), preferred_element_type=jnp.float32)
    return (g_img, g_txt)

def finish(inverse, normed, grads):
    return inverse * (grads - normed * lax.optimization_barrier(jnp.sum(normed * grads, axis=1, keepdims=True)))

def reference(image_emb, text_emb, scale, bias):
    img_inv, img_norm = unit_rows(image_emb)
    txt_inv, txt_norm = unit_rows(text_emb)
    img_unit = img_norm.astype(jnp.bfloat16)
    txt_unit = txt_norm.astype(jnp.bfloat16)
    block_rows = TOKENS // N_ROW
    starts = (jnp.arange(N_ROW) * block_rows).astype(jnp.int32)

    def step(g_txt, start):
        block = lax.dynamic_slice_in_dim(img_unit, start, block_rows, 0)
        g_img, g_part = tile_terms(block, txt_unit, start, jnp.zeros((), jnp.int32), scale[0], bias[0])
        return (g_txt + g_part, g_img)
    g_txt, g_blocks = lax.scan(step, jnp.zeros((TOKENS, D), jnp.float32), starts)
    g_img = g_blocks.reshape(TOKENS, D)
    grad_image = finish(img_inv, img_norm, g_img)
    grad_text = finish(txt_inv, txt_norm, g_txt)
    return (grad_image, grad_text)
```

```python
import jax
import jax.numpy as jnp
from jax import lax
from jax.experimental import pallas as pl
from jax.experimental.pallas import tpu as pltpu
from jax.sharding import PartitionSpec as P

MESH = pl.DeviceIdType.MESH
F32 = jnp.float32
BF16 = jnp.bfloat16
SHARD = 128
PARTS = ((0, 48), (48, 48), (96, 32))
ORDER = (0, 2, 1, 3, 5, 7, 4, 6)
SLOT = {position: slot for slot, position in enumerate(ORDER)}


def dot(a, b, contract):
    return lax.dot_general(a, b, (contract, ((), ())), preferred_element_type=F32)


def unit_rows(raw):
    values = raw.astype(F32)
    inverse = lax.rsqrt(jnp.sum(values * values, axis=1, keepdims=True) + 1e-06)
    return (inverse, values * inverse)


def low_bit(position):
    return next(s for s in range(3) if position >> s & 1)


def high_bit(position):
    return max(s for s in range(3) if position >> s & 1)


class Place:
    def __init__(self):
        row, col = lax.axis_index("row"), lax.axis_index("col")
        self.core = lax.rem(row, 2)
        x = lax.rem(col, 2) * 2 + lax.rem(lax.div(row, 2), 2)
        self.chip = (x, lax.div(col, 2), lax.div(row, 4))
        even = tuple(c + 1 - 2 * lax.rem(c, 2) for c in self.chip)
        odd = tuple(lax.rem(c + 3 + 2 * lax.rem(c, 2), 4) for c in self.chip)
        self.partner = (even, odd)

    def device(self, chip, core):
        x, y, z = chip
        return (z * 4 + lax.rem(x, 2) * 2 + core, y * 2 + lax.div(x, 2))

    def sibling(self):
        return self.device(self.chip, 1 - self.core)

    def neighbour(self, kind, axis):
        chip = list(self.chip)
        chip[axis] = self.partner[kind][axis]
        return self.device(chip, self.core)

    def along(self, kind, part, step):
        a = self.neighbour(kind, (part + step) % 3)
        b = self.neighbour(kind, (part + step + 1) % 3)
        return tuple(u + self.core * (v - u) for u, v in zip(a, b))

    def shard(self, kind, part, position, core):
        chip = []
        for axis in range(3):
            f0 = position >> ((axis - part) % 3) & 1
            f1 = position >> ((axis - part - 1) % 3) & 1
            flip = f0 + core * (f1 - f0)
            chip.append(self.chip[axis] + flip * (self.partner[kind][axis] - self.chip[axis]))
        row, col = self.device(chip, core)
        return row * 8 + col if kind == 0 else col * 16 + row


def kernel(
    scale_ref, bias_ref, image_ref, text_ref, grad_image_ref, grad_text_ref,
    img, txt, g_img, g_txt, img_out, img_in, txt_out, txt_in, sib_out, sib_in, img_id, txt_id,
    gather_send, gather_recv, pair_send, pair_recv, reduce_send, reduce_recv, back_send, back_recv,
):
    place = Place()
    sibling = place.sibling()
    links = [place.neighbour(kind, axis) for kind in range(2) for axis in range(3)]
    hops = [[[place.along(kind, p, s) for s in range(3)] for p in range(3)] for kind in range(2)]

    barrier = pltpu.get_barrier_semaphore()
    for other in links + [sibling]:
        pl.semaphore_signal(barrier, inc=1, device_id=other, device_id_type=MESH)

    image_inverse, image_norm = unit_rows(image_ref[...])
    img[0:SHARD, :] = image_norm.astype(BF16)
    text_inverse, text_norm = unit_rows(text_ref[...])
    txt[0:SHARD, :] = text_norm.astype(BF16)
    scale = scale_ref[0]
    bias = bias_ref[0]

    pl.semaphore_wait(barrier, len(links) + 1)

    held = (img, txt)
    outs, ins = (img_out, txt_out), (img_in, txt_in)
    stride = (SHARD, 2 * SHARD)

    def rows(ref, kind, position, part=None, side=0, step=None):
        first = SLOT[position] * (stride[kind] if step is None else step) + side * SHARD
        if part is None:
            return ref.at[pl.ds(first, SHARD)]
        return ref.at[pl.ds(first + PARTS[part][0], PARTS[part][1])]

    def remote(src, dst, send, recv, device):
        return pltpu.make_async_remote_copy(
            src_ref=src, dst_ref=dst, send_sem=send, recv_sem=recv, device_id=device, device_id_type=MESH
        )

    def pass_on(kind, position, step):
        target = position + (1 << step)
        for p in range(3):
            remote(
                rows(held[kind], kind, position, p), rows(held[kind], kind, target, p),
                gather_send.at[kind, target], gather_recv.at[kind, target], hops[kind][p][step],
            ).start()

    def gathered(kind, position):
        whole = rows(held[kind], kind, position)
        return remote(whole, whole, gather_send.at[kind, position], gather_recv.at[kind, position], sibling)

    def pair_copy(position):
        return remote(
            rows(txt, 1, position), rows(txt, 1, position, side=1),
            pair_send.at[position], pair_recv.at[position], sibling,
        )

    def reduced(kind, position):
        return remote(
            rows(outs[kind], kind, position, step=SHARD), rows(ins[kind], kind, position, step=SHARD),
            reduce_send.at[kind, position], reduce_recv.at[kind, position], sibling,
        )

    def back_copy(position):
        return remote(
            rows(sib_out, 1, position, step=SHARD), rows(sib_in, 1, position, step=SHARD),
            back_send.at[position], back_recv.at[position], sibling,
        )

    for step in (0, 1):
        for kind in (0, 1):
            pass_on(kind, 0, step)
    pair_copy(0).start()

    g_img[...] = jnp.zeros_like(g_img)
    g_txt[...] = jnp.zeros_like(g_txt)
    down = lax.broadcasted_iota(jnp.int32, (SHARD, 128), 0)
    across = lax.broadcasted_iota(jnp.int32, (8, SHARD), 1)

    def numbers(index, kind, position, core):
        a, b, c = (place.shard(kind, p, position, core) * SHARD for p in range(3))
        return index + jnp.where(index < PARTS[1][0], a, jnp.where(index < PARTS[2][0], b, c))

    for position in range(8):
        first = SLOT[position] * SHARD
        img_id[first : first + SHARD, :] = numbers(down, 0, position, place.core)
        for side, core in enumerate((place.core, 1 - place.core)):
            begin = SLOT[position] * 2 * SHARD + side * SHARD
            txt_id[:, begin : begin + SHARD] = numbers(across, 1, position, core)

    for kind in (0, 1):
        gathered(kind, 1).wait_recv()
        pass_on(kind, 1, 1)
    for kind in (0, 1):
        pass_on(kind, 1, 2)
    pair_copy(1).start()
    for position in (3, 2):
        for kind in (1, 0):
            gathered(kind, position).wait_recv()
        for kind in (1, 0):
            pass_on(kind, position, 2)
            if position == 3:
                pass_on(kind, 0, 2)
        pair_copy(position).start()

    def block(a, a_count, b):
        r = pl.ds(a * 2 * SHARD, a_count * 2 * SHARD)
        c = pl.ds(b * 4 * SHARD, 4 * SHARD)
        sims = dot(img[r, :], txt[c, :], ((1,), (1,)))
        same = img_id[r, 0:1] == txt_id[0:1, c]
        logits = scale * sims + bias
        coef = scale / (1.0 + jnp.exp(jnp.where(same, logits, -logits)))
        coef = jnp.where(same, -coef, coef).astype(BF16)
        g_img[r, :] += dot(coef, txt[c, :], ((1,), (0,)))
        g_txt[c, :] += dot(coef, img[r, :], ((0,), (0,)))

    def paired(*positions):
        for position in positions:
            pair_copy(position).wait_recv()

    def arrive(kind, *positions):
        for position in positions:
            gathered(kind, position).wait_recv()
            if kind == 1:
                pair_copy(position).start()

    def give_back(*positions):
        for position in positions:
            other = rows(g_txt, 1, position, side=1)
            rows(sib_out, 1, position, step=SHARD)[...] = other[...].astype(BF16)
            back_copy(position).start()

    def total(kind, position):
        value = rows((g_img, g_txt)[kind], kind, position)[...]
        if kind == 1:
            back_copy(position).wait_recv()
            value += rows(sib_in, 1, position, step=SHARD)[...].astype(F32)
        for s in range(3 if position == 0 else low_bit(position)):
            child = position + (1 << s)
            reduced(kind, child).wait_recv()
            value += rows(ins[kind], kind, child, step=SHARD)[...].astype(F32)
        return value

    def hand_on(kind, *positions):
        for position in positions:
            rows(outs[kind], kind, position, step=SHARD)[...] = total(kind, position).astype(BF16)
            for p in range(3):
                remote(
                    rows(outs[kind], kind, position, p, step=SHARD), rows(ins[kind], kind, position, p, step=SHARD),
                    reduce_send.at[kind, position], reduce_recv.at[kind, position],
                    hops[kind][p][low_bit(position)],
                ).start()

    paired(0, 2)
    block(0, 2, 0)
    arrive(1, 5)
    paired(1, 3)
    block(0, 2, 1)
    arrive(1, 7)
    arrive(0, 5, 7)
    block(2, 1, 0)
    arrive(1, 4)
    paired(5, 7)
    block(0, 2, 2)
    arrive(1, 6)
    arrive(0, 4, 6)
    block(2, 2, 1)
    give_back(1, 3)
    block(2, 2, 2)
    give_back(5, 7)
    hand_on(1, 1, 3)
    paired(4, 6)
    block(1, 2, 3)
    hand_on(1, 5, 7)
    hand_on(0, 1, 3, 5, 7)
    block(3, 1, 3)
    block(0, 1, 3)
    give_back(6, 4)
    block(3, 1, 0)
    give_back(2, 0)
    hand_on(1, 6)
    hand_on(0, 6)
    hand_on(1, 2)
    hand_on(0, 2)
    hand_on(1, 4)
    hand_on(0, 4)

    def finish(inverse, normed, grads):
        return inverse * (grads - normed * jnp.sum(normed * grads, axis=1, keepdims=True))

    text_inverse, text_norm = unit_rows(text_ref[...])
    grad_text_ref[...] = finish(text_inverse, text_norm, total(1, 0))
    image_inverse, image_norm = unit_rows(image_ref[...])
    grad_image_ref[...] = finish(image_inverse, image_norm, total(0, 0))

    for position in range(8):
        pair_copy(position).wait_send()
        back_copy(position).wait_send()
        if position:
            for kind in (0, 1):
                gathered(kind, position).wait_send()
                reduced(kind, position).wait_send()


def per_device(image_emb, text_emb, scale, bias):
    width = image_emb.shape[1]
    vmem = pl.BlockSpec(memory_space=pltpu.VMEM)
    smem = pl.BlockSpec(memory_space=pltpu.SMEM)
    dma = pltpu.SemaphoreType.DMA
    whole = 8 * SHARD
    out = jax.ShapeDtypeStruct((SHARD, width), F32)
    return pl.pallas_call(
        kernel,
        out_shape=(out, out),
        in_specs=[smem, smem, vmem, vmem],
        out_specs=(vmem, vmem),
        scratch_shapes=[
            pltpu.VMEM((whole, width), BF16),
            pltpu.VMEM((2 * whole, width), BF16),
            pltpu.VMEM((whole, width), F32),
            pltpu.VMEM((2 * whole, width), F32),
            *[pltpu.VMEM((whole, width), BF16) for _ in range(6)],
            pltpu.VMEM((whole, 128), jnp.int32),
            pltpu.VMEM((8, 2 * whole), jnp.int32),
            dma((2, 8)), dma((2, 8)), dma((8,)), dma((8,)),
            dma((2, 8)), dma((2, 8)), dma((8,)), dma((8,)),
        ],
        compiler_params=pltpu.CompilerParams(
            collective_id=0, has_side_effects=True, vmem_limit_bytes=60 * 2**20
        ),
        cost_estimate=pl.CostEstimate(
            flops=6 * 2 * whole * whole * width, bytes_accessed=12 * SHARD * width, transcendentals=2 * whole * whole
        ),
    )(scale, bias, image_emb, text_emb)


def solution(mesh):
    placed = (P(("row", "col"), None), P(("col", "row"), None), P(), P())
    return jax.shard_map(
        per_device,
        mesh=mesh,
        in_specs=placed,
        out_specs=(P(("row", "col"), None), P(("col", "row"), None)),
        check_vma=False,
    )
```

```python
import jax
import jax.numpy as jnp
from jax import lax
from jax.experimental import pallas as pl
from jax.experimental.pallas import tpu as pltpu
from jax.sharding import PartitionSpec as P

MESH = pl.DeviceIdType.MESH
F32 = jnp.float32
BF16 = jnp.bfloat16
SHARD = 128
PARTS = ((0, 48), (48, 48), (96, 32))
ORDER = (0, 4, 1, 2, 3, 5, 6, 7)
SLOT = {position: slot for slot, position in enumerate(ORDER)}


def dot(a, b, contract):
    return lax.dot_general(a, b, (contract, ((), ())), preferred_element_type=F32)


def unit_rows(raw):
    values = raw.astype(F32)
    inverse = lax.rsqrt(jnp.sum(values * values, axis=1, keepdims=True) + 1e-06)
    return (inverse, values * inverse)


def low_bit(position):
    return next(s for s in range(3) if position >> s & 1)


def high_bit(position):
    return max(s for s in range(3) if position >> s & 1)


def text_row(position, side):
    slot = SLOT[position]
    if slot < 4:
        return (side * 4 + slot) * SHARD
    return (slot // 2 * 4 + side * 2 + slot % 2) * SHARD


class Place:
    def __init__(self):
        row, col = lax.axis_index("row"), lax.axis_index("col")
        self.core = lax.rem(row, 2)
        x = lax.rem(col, 2) * 2 + lax.rem(lax.div(row, 2), 2)
        self.chip = (x, lax.div(col, 2), lax.div(row, 4))
        even = tuple(c + 1 - 2 * lax.rem(c, 2) for c in self.chip)
        odd = tuple(lax.rem(c + 3 + 2 * lax.rem(c, 2), 4) for c in self.chip)
        self.partner = (even, odd)

    def device(self, chip, core):
        x, y, z = chip
        return (z * 4 + lax.rem(x, 2) * 2 + core, y * 2 + lax.div(x, 2))

    def sibling(self):
        return self.device(self.chip, 1 - self.core)

    def neighbour(self, kind, axis):
        chip = list(self.chip)
        chip[axis] = self.partner[kind][axis]
        return self.device(chip, self.core)

    def along(self, kind, part, step):
        a = self.neighbour(kind, (part + step) % 3)
        b = self.neighbour(kind, (part + step + 1) % 3)
        return tuple(u + self.core * (v - u) for u, v in zip(a, b))

    def shard(self, kind, part, position, core):
        chip = []
        for axis in range(3):
            f0 = position >> ((axis - part) % 3) & 1
            f1 = position >> ((axis - part - 1) % 3) & 1
            flip = f0 + core * (f1 - f0)
            chip.append(self.chip[axis] + flip * (self.partner[kind][axis] - self.chip[axis]))
        row, col = self.device(chip, core)
        return row * 8 + col if kind == 0 else col * 16 + row


def kernel(
    scale_hbm, bias_hbm, image_hbm, text_hbm, grad_image_ref, grad_text_ref,
    scale_ref, bias_ref, image_ref, text_ref, load, img, txt, g_img, g_txt, img_out, img_in, txt_out, txt_in, sib_out, sib_in, img_id, txt_id,
    gather_send, gather_recv, pair_send, pair_recv, reduce_send, reduce_recv, back_send, back_recv,
):
    place = Place()
    sibling = place.sibling()
    links = [place.neighbour(kind, axis) for kind in range(2) for axis in range(3)]
    barrier = pltpu.get_barrier_semaphore()
    for other in links + [sibling]:
        pl.semaphore_signal(barrier, inc=1, device_id=other, device_id_type=MESH)

    loads = [
        pltpu.make_async_copy(src, dst, load.at[i])
        for i, (src, dst) in enumerate(
            ((image_hbm, image_ref), (text_hbm, text_ref), (scale_hbm, scale_ref), (bias_hbm, bias_ref))
        )
    ]
    for copy in loads:
        copy.start()
    hops = [[[place.along(kind, p, s) for s in range(3)] for p in range(3)] for kind in range(2)]

    held = (img, txt)
    outs, ins = (img_out, txt_out), (img_in, txt_in)

    def rows(ref, kind, position, part=None, side=0, packed=False):
        first = SLOT[position] * SHARD if packed or kind == 0 else text_row(position, side)
        if part is None:
            return ref.at[pl.ds(first, SHARD)]
        return ref.at[pl.ds(first + PARTS[part][0], PARTS[part][1])]

    def remote(src, dst, send, recv, device):
        return pltpu.make_async_remote_copy(
            src_ref=src, dst_ref=dst, send_sem=send, recv_sem=recv, device_id=device, device_id_type=MESH
        )

    def pass_on(kind, position, step):
        target = position + (1 << step)
        for p in range(3):
            remote(
                rows(held[kind], kind, position, p), rows(held[kind], kind, target, p),
                gather_send.at[kind, target], gather_recv.at[kind, target], hops[kind][p][step],
            ).start()

    def gathered(kind, position):
        whole = rows(held[kind], kind, position)
        return remote(whole, whole, gather_send.at[kind, position], gather_recv.at[kind, position], sibling)

    def pair_copy(position):
        return remote(
            rows(txt, 1, position), rows(txt, 1, position, side=1),
            pair_send.at[position], pair_recv.at[position], sibling,
        )

    def reduced(kind, position):
        return remote(
            rows(outs[kind], kind, position, packed=True), rows(ins[kind], kind, position, packed=True),
            reduce_send.at[kind, position], reduce_recv.at[kind, position], sibling,
        )

    def back_copy(position):
        return remote(
            rows(sib_out, 1, position, packed=True), rows(sib_in, 1, position, packed=True),
            back_send.at[position], back_recv.at[position], sibling,
        )

    for kind, raw in ((1, text_ref), (0, image_ref)):
        loads[kind].wait()
        held[kind][0:SHARD, :] = unit_rows(raw[...])[1].astype(BF16)
        if kind == 1:
            pl.semaphore_wait(barrier, len(links) + 1)
        for step in range(3):
            pass_on(kind, 0, step)
    pair_copy(0).start()
    loads[2].wait()
    loads[3].wait()
    scale = scale_ref[0]
    bias = bias_ref[0]

    g_img[...] = jnp.zeros_like(g_img)
    g_txt[...] = jnp.zeros_like(g_txt)
    down = lax.broadcasted_iota(jnp.int32, (SHARD, 128), 0)
    across = lax.broadcasted_iota(jnp.int32, (8, SHARD), 1)

    def numbers(index, kind, position, core):
        a, b, c = (place.shard(kind, p, position, core) * SHARD for p in range(3))
        return index + jnp.where(index < PARTS[1][0], a, jnp.where(index < PARTS[2][0], b, c))

    for position in range(8):
        first = SLOT[position] * SHARD
        img_id[first : first + SHARD, :] = numbers(down, 0, position, place.core)
        for side, core in enumerate((place.core, 1 - place.core)):
            begin = text_row(position, side)
            txt_id[:, begin : begin + SHARD] = numbers(across, 1, position, core)

    for position in (1, 2):
        for kind in (1, 0):
            gathered(kind, position).wait_recv()
            for step in range(position, 3):
                pass_on(kind, position, step)
        pair_copy(position).start()
    for kind in (1, 0):
        gathered(kind, 4).wait_recv()
    pair_copy(4).start()

    def block(a, a_count, b):
        r = pl.ds(a * 2 * SHARD, a_count * 2 * SHARD)
        c = pl.ds(b * 4 * SHARD, 4 * SHARD)
        sims = dot(img[r, :], txt[c, :], ((1,), (1,)))
        same = img_id[r, 0:1] == txt_id[0:1, c]
        odds = jnp.exp(-scale * sims - bias)
        coef = scale / (1.0 + odds)
        coef = (coef * jnp.where(same, -odds, 1.0)).astype(BF16)
        g_img[r, :] += dot(coef, txt[c, :], ((1,), (0,)))
        g_txt[c, :] += dot(coef, img[r, :], ((0,), (0,)))

    def paired(*positions):
        for position in positions:
            pair_copy(position).wait_recv()

    def arrive(kind, *positions):
        for position in positions:
            gathered(kind, position).wait_recv()
            if position == 3:
                pass_on(kind, 3, 2)
            if kind == 1:
                pair_copy(position).start()

    def give_back(*positions):
        for position in positions:
            other = rows(g_txt, 1, position, side=1)
            rows(sib_out, 1, position, packed=True)[...] = other[...].astype(BF16)
            back_copy(position).start()

    def total(kind, position):
        value = rows((g_img, g_txt)[kind], kind, position)[...]
        if kind == 1:
            back_copy(position).wait_recv()
            value += rows(sib_in, 1, position, packed=True)[...].astype(F32)
        for s in range(3 if position == 0 else low_bit(position)):
            child = position + (1 << s)
            reduced(kind, child).wait_recv()
            value += rows(ins[kind], kind, child, packed=True)[...].astype(F32)
        return value

    def hand_on(kind, *positions):
        for position in positions:
            rows(outs[kind], kind, position, packed=True)[...] = total(kind, position).astype(BF16)
            for p in range(3):
                remote(
                    rows(outs[kind], kind, position, p, packed=True), rows(ins[kind], kind, position, p, packed=True),
                    reduce_send.at[kind, position], reduce_recv.at[kind, position],
                    hops[kind][p][low_bit(position)],
                ).start()

    block(0, 2, 0)
    arrive(1, 3)
    arrive(0, 3)
    paired(0, 1, 2, 4)
    block(0, 2, 1)
    arrive(1, 5)
    arrive(0, 5)
    block(2, 1, 0)
    block(2, 1, 1)
    arrive(1, 6)
    paired(3, 5)
    block(0, 2, 2)
    arrive(1, 7)
    arrive(0, 6, 7)
    block(2, 2, 2)
    give_back(3, 5)
    paired(6, 7)
    block(0, 2, 3)
    hand_on(0, 1)
    hand_on(1, 3, 5)
    block(2, 2, 3)
    give_back(7, 6)
    hand_on(0, 3, 5)
    block(3, 1, 1)
    give_back(1, 2, 4, 0)
    hand_on(1, 7)
    block(3, 1, 0)
    hand_on(0, 7)
    hand_on(1, 1)
    hand_on(0, 2)
    hand_on(1, 2)
    hand_on(1, 6)
    hand_on(0, 6)
    hand_on(1, 4)
    hand_on(0, 4)

    def finish(inverse, normed, grads):
        return inverse * (grads - normed * jnp.sum(normed * grads, axis=1, keepdims=True))

    text_inverse, text_norm = unit_rows(text_ref[...])
    grad_text_ref[...] = finish(text_inverse, text_norm, total(1, 0))
    image_inverse, image_norm = unit_rows(image_ref[...])
    grad_image_ref[...] = finish(image_inverse, image_norm, total(0, 0))

    for position in range(8):
        pair_copy(position).wait_send()
        back_copy(position).wait_send()
        if position:
            for kind in (0, 1):
                gathered(kind, position).wait_send()
                reduced(kind, position).wait_send()


def per_device(image_emb, text_emb, scale, bias):
    width = image_emb.shape[1]
    vmem = pl.BlockSpec(memory_space=pltpu.VMEM)
    dma = pltpu.SemaphoreType.DMA
    whole = 8 * SHARD
    out = jax.ShapeDtypeStruct((SHARD, width), F32)
    return pl.pallas_call(
        kernel,
        out_shape=(out, out),
        in_specs=[pl.BlockSpec(memory_space=pl.ANY)] * 4,
        out_specs=(vmem, vmem),
        scratch_shapes=[
            pltpu.SMEM((1,), F32),
            pltpu.SMEM((1,), F32),
            pltpu.VMEM((SHARD, width), BF16),
            pltpu.VMEM((SHARD, width), BF16),
            dma((4,)),
            pltpu.VMEM((whole, width), BF16),
            pltpu.VMEM((2 * whole, width), BF16),
            pltpu.VMEM((whole, width), F32),
            pltpu.VMEM((2 * whole, width), F32),
            *[pltpu.VMEM((whole, width), BF16) for _ in range(6)],
            pltpu.VMEM((whole, 128), jnp.int32),
            pltpu.VMEM((8, 2 * whole), jnp.int32),
            dma((2, 8)), dma((2, 8)), dma((8,)), dma((8,)),
            dma((2, 8)), dma((2, 8)), dma((8,)), dma((8,)),
        ],
        compiler_params=pltpu.CompilerParams(
            collective_id=0, has_side_effects=True, vmem_limit_bytes=50 * 2**20
        ),
        cost_estimate=pl.CostEstimate(
            flops=6 * 2 * whole * whole * width, bytes_accessed=12 * SHARD * width, transcendentals=2 * whole * whole
        ),
    )(scale, bias, image_emb, text_emb)


def solution(mesh):
    placed = (P(("row", "col"), None), P(("col", "row"), None), P(), P())
    return jax.shard_map(
        per_device,
        mesh=mesh,
        in_specs=placed,
        out_specs=(P(("row", "col"), None), P(("col", "row"), None)),
        check_vma=False,
    )
```

```python
import jax
import jax.numpy as jnp
from jax import lax
from jax.experimental import pallas as pl
from jax.experimental.pallas import tpu as pltpu
from jax.sharding import PartitionSpec as P

MESH = pl.DeviceIdType.MESH
F32 = jnp.float32
BF16 = jnp.bfloat16
SHARD = 128
PARTS = ((0, 48), (48, 48), (96, 32))
ORDER = (0, 4, 1, 2, 3, 5, 6, 7)
SLOT = {position: slot for slot, position in enumerate(ORDER)}


def dot(a, b, contract):
    return lax.dot_general(a, b, (contract, ((), ())), preferred_element_type=F32)


def unit_rows(raw):
    values = raw.astype(F32)
    inverse = lax.rsqrt(jnp.sum(values * values, axis=1, keepdims=True) + 1e-06)
    return (inverse, values * inverse)


def low_bit(position):
    return next(s for s in range(3) if position >> s & 1)


def high_bit(position):
    return max(s for s in range(3) if position >> s & 1)


def text_row(position, side):
    slot = SLOT[position]
    if slot < 4:
        return (side * 4 + slot) * SHARD
    return (slot // 2 * 4 + side * 2 + slot % 2) * SHARD


class Place:
    def __init__(self):
        row, col = lax.axis_index("row"), lax.axis_index("col")
        self.core = lax.rem(row, 2)
        x = lax.rem(col, 2) * 2 + lax.rem(lax.div(row, 2), 2)
        self.chip = (x, lax.div(col, 2), lax.div(row, 4))
        even = tuple(c + 1 - 2 * lax.rem(c, 2) for c in self.chip)
        odd = tuple(lax.rem(c + 3 + 2 * lax.rem(c, 2), 4) for c in self.chip)
        self.partner = (even, odd)

    def device(self, chip, core):
        x, y, z = chip
        return (z * 4 + lax.rem(x, 2) * 2 + core, y * 2 + lax.div(x, 2))

    def sibling(self):
        return self.device(self.chip, 1 - self.core)

    def neighbour(self, kind, axis):
        chip = list(self.chip)
        chip[axis] = self.partner[kind][axis]
        return self.device(chip, self.core)

    def along(self, kind, part, step):
        a = self.neighbour(kind, (part + step) % 3)
        b = self.neighbour(kind, (part + step + 1) % 3)
        return tuple(u + self.core * (v - u) for u, v in zip(a, b))

    def shard(self, kind, part, position, core):
        chip = []
        for axis in range(3):
            f0 = position >> ((axis - part) % 3) & 1
            f1 = position >> ((axis - part - 1) % 3) & 1
            flip = f0 + core * (f1 - f0)
            chip.append(self.chip[axis] + flip * (self.partner[kind][axis] - self.chip[axis]))
        row, col = self.device(chip, core)
        return row * 8 + col if kind == 0 else col * 16 + row


def kernel(
    scale_hbm, bias_hbm, image_hbm, text_hbm, grad_image_ref, grad_text_ref,
    scale_ref, bias_ref, image_ref, text_ref, load, img, txt, g_img, g_txt, img_out, img_in, txt_out, txt_in, sib_out, sib_in, img_id, txt_id,
    gather_send, gather_recv, pair_send, pair_recv, reduce_send, reduce_recv, back_send, back_recv,
):
    place = Place()
    sibling = place.sibling()
    links = [place.neighbour(kind, axis) for kind in range(2) for axis in range(3)]
    barrier = pltpu.get_barrier_semaphore()
    for other in links + [sibling]:
        pl.semaphore_signal(barrier, inc=1, device_id=other, device_id_type=MESH)

    loads = [
        pltpu.make_async_copy(src, dst, load.at[i])
        for i, (src, dst) in enumerate(
            ((image_hbm, image_ref), (text_hbm, text_ref), (scale_hbm, scale_ref), (bias_hbm, bias_ref))
        )
    ]
    for copy in loads:
        copy.start()
    hops = [[[place.along(kind, p, s) for s in range(3)] for p in range(3)] for kind in range(2)]

    held = (img, txt)
    outs, ins = (img_out, txt_out), (img_in, txt_in)

    def rows(ref, kind, position, part=None, side=0, packed=False):
        first = SLOT[position] * SHARD if packed or kind == 0 else text_row(position, side)
        if part is None:
            return ref.at[pl.ds(first, SHARD)]
        return ref.at[pl.ds(first + PARTS[part][0], PARTS[part][1])]

    def remote(src, dst, send, recv, device):
        return pltpu.make_async_remote_copy(
            src_ref=src, dst_ref=dst, send_sem=send, recv_sem=recv, device_id=device, device_id_type=MESH
        )

    def pass_on(kind, position, step):
        target = position + (1 << step)
        for p in range(3):
            remote(
                rows(held[kind], kind, position, p), rows(held[kind], kind, target, p),
                gather_send.at[kind, target], gather_recv.at[kind, target], hops[kind][p][step],
            ).start()

    def gathered(kind, position):
        whole = rows(held[kind], kind, position)
        return remote(whole, whole, gather_send.at[kind, position], gather_recv.at[kind, position], sibling)

    def pair_copy(position):
        return remote(
            rows(txt, 1, position), rows(txt, 1, position, side=1),
            pair_send.at[position], pair_recv.at[position], sibling,
        )

    def reduced(kind, position):
        return remote(
            rows(outs[kind], kind, position, packed=True), rows(ins[kind], kind, position, packed=True),
            reduce_send.at[kind, position], reduce_recv.at[kind, position], sibling,
        )

    def back_copy(position):
        return remote(
            rows(sib_out, 1, position, packed=True), rows(sib_in, 1, position, packed=True),
            back_send.at[position], back_recv.at[position], sibling,
        )

    for kind, raw in ((1, text_ref), (0, image_ref)):
        loads[kind].wait()
        held[kind][0:SHARD, :] = unit_rows(raw[...])[1].astype(BF16)
        if kind == 1:
            pl.semaphore_wait(barrier, len(links) + 1)
        for step in range(3):
            pass_on(kind, 0, step)
    pair_copy(0).start()
    loads[2].wait()
    loads[3].wait()
    scale = scale_ref[0]
    bias = bias_ref[0]

    g_img[...] = jnp.zeros_like(g_img)
    g_txt[...] = jnp.zeros_like(g_txt)
    down = lax.broadcasted_iota(jnp.int32, (SHARD, 128), 0)
    across = lax.broadcasted_iota(jnp.int32, (8, SHARD), 1)

    def numbers(index, kind, position, core):
        a, b, c = (place.shard(kind, p, position, core) * SHARD for p in range(3))
        return index + jnp.where(index < PARTS[1][0], a, jnp.where(index < PARTS[2][0], b, c))

    for position in range(8):
        first = SLOT[position] * SHARD
        img_id[first : first + SHARD, :] = numbers(down, 0, position, place.core)
        for side, core in enumerate((place.core, 1 - place.core)):
            begin = text_row(position, side)
            txt_id[:, begin : begin + SHARD] = numbers(across, 1, position, core)

    for position in (1, 2):
        for kind in (1, 0):
            gathered(kind, position).wait_recv()
            for step in range(position, 3):
                pass_on(kind, position, step)
        pair_copy(position).start()
    for kind in (1, 0):
        gathered(kind, 4).wait_recv()
    pair_copy(4).start()

    def block(a, a_count, b):
        r = pl.ds(a * 2 * SHARD, a_count * 2 * SHARD)
        c = pl.ds(b * 4 * SHARD, 4 * SHARD)
        sims = dot(img[r, :], txt[c, :], ((1,), (1,)))
        same = img_id[r, 0:1] == txt_id[0:1, c]
        odds = jnp.exp(-scale * sims - bias)
        coef = scale / (1.0 + odds)
        coef = (coef * jnp.where(same, -odds, 1.0)).astype(BF16)
        g_img[r, :] += dot(coef, txt[c, :], ((1,), (0,)))
        g_txt[c, :] += dot(coef, img[r, :], ((0,), (0,)))

    def paired(*positions):
        for position in positions:
            pair_copy(position).wait_recv()

    def arrive(kind, *positions):
        for position in positions:
            gathered(kind, position).wait_recv()
            if position == 3:
                pass_on(kind, 3, 2)
            if kind == 1:
                pair_copy(position).start()

    def give_back(*positions):
        for position in positions:
            other = rows(g_txt, 1, position, side=1)
            rows(sib_out, 1, position, packed=True)[...] = other[...].astype(BF16)
            back_copy(position).start()

    def total(kind, position):
        value = rows((g_img, g_txt)[kind], kind, position)[...]
        if kind == 1:
            back_copy(position).wait_recv()
            value += rows(sib_in, 1, position, packed=True)[...].astype(F32)
        for s in range(3 if position == 0 else low_bit(position)):
            child = position + (1 << s)
            reduced(kind, child).wait_recv()
            value += rows(ins[kind], kind, child, packed=True)[...].astype(F32)
        return value

    def hand_on(kind, *positions):
        for position in positions:
            rows(outs[kind], kind, position, packed=True)[...] = total(kind, position).astype(BF16)
            for p in range(3):
                remote(
                    rows(outs[kind], kind, position, p, packed=True), rows(ins[kind], kind, position, p, packed=True),
                    reduce_send.at[kind, position], reduce_recv.at[kind, position],
                    hops[kind][p][low_bit(position)],
                ).start()

    block(0, 2, 0)
    arrive(1, 3)
    arrive(0, 3)
    paired(0, 1, 2, 4)
    block(0, 2, 1)
    arrive(1, 5)
    arrive(0, 5)
    block(2, 1, 0)
    block(2, 1, 1)
    arrive(1, 6)
    paired(3, 5)
    block(0, 2, 2)
    arrive(1, 7)
    arrive(0, 6, 7)
    block(2, 2, 2)
    give_back(3, 5)
    paired(6, 7)
    block(0, 2, 3)
    hand_on(0, 1)
    hand_on(1, 3, 5)
    block(2, 2, 3)
    give_back(7, 6)
    hand_on(0, 3, 5)
    block(3, 1, 1)
    give_back(1, 2, 4, 0)
    hand_on(1, 7)
    block(3, 1, 0)
    hand_on(0, 7)
    hand_on(1, 1)
    hand_on(0, 2)
    hand_on(1, 2)
    hand_on(1, 6)
    hand_on(0, 6)
    hand_on(1, 4)
    hand_on(0, 4)

    def finish(inverse, normed, grads):
        return inverse * (grads - normed * jnp.sum(normed * grads, axis=1, keepdims=True))

    text_inverse, text_norm = unit_rows(text_ref[...])
    image_inverse, image_norm = unit_rows(image_ref[...])
    grad_text_ref[...] = finish(text_inverse, text_norm, total(1, 0))
    grad_image_ref[...] = finish(image_inverse, image_norm, total(0, 0))

    for position in range(8):
        pair_copy(position).wait_send()
        back_copy(position).wait_send()
        if position:
            for kind in (0, 1):
                gathered(kind, position).wait_send()
                reduced(kind, position).wait_send()


def per_device(image_emb, text_emb, scale, bias):
    width = image_emb.shape[1]
    vmem = pl.BlockSpec(memory_space=pltpu.VMEM)
    dma = pltpu.SemaphoreType.DMA
    whole = 8 * SHARD
    out = jax.ShapeDtypeStruct((SHARD, width), F32)
    return pl.pallas_call(
        kernel,
        out_shape=(out, out),
        in_specs=[pl.BlockSpec(memory_space=pl.ANY)] * 4,
        out_specs=(vmem, vmem),
        scratch_shapes=[
            pltpu.SMEM((1,), F32),
            pltpu.SMEM((1,), F32),
            pltpu.VMEM((SHARD, width), BF16),
            pltpu.VMEM((SHARD, width), BF16),
            dma((4,)),
            pltpu.VMEM((whole, width), BF16),
            pltpu.VMEM((2 * whole, width), BF16),
            pltpu.VMEM((whole, width), F32),
            pltpu.VMEM((2 * whole, width), F32),
            *[pltpu.VMEM((whole, width), BF16) for _ in range(6)],
            pltpu.VMEM((whole, 128), jnp.int32),
            pltpu.VMEM((8, 2 * whole), jnp.int32),
            dma((2, 8)), dma((2, 8)), dma((8,)), dma((8,)),
            dma((2, 8)), dma((2, 8)), dma((8,)), dma((8,)),
        ],
        compiler_params=pltpu.CompilerParams(
            collective_id=0, has_side_effects=True, vmem_limit_bytes=50 * 2**20
        ),
        cost_estimate=pl.CostEstimate(
            flops=6 * 2 * whole * whole * width, bytes_accessed=12 * SHARD * width, transcendentals=2 * whole * whole
        ),
    )(scale, bias, image_emb, text_emb)


def solution(mesh):
    placed = (P(("row", "col"), None), P(("col", "row"), None), P(), P())
    return jax.shard_map(
        per_device,
        mesh=mesh,
        in_specs=placed,
        out_specs=(P(("row", "col"), None), P(("col", "row"), None)),
        check_vma=False,
    )
```
